32 devices in a mesh: blk: 8 (over y, x, core), rep: 4 (over z).
Axes of the slice: x: 2, y: 2, z: 4, core: 2. Of those that a mesh axis runs over, the one named last changes fastest.
Arguments:
- entities: bfloat16 [16384, 256], P('blk'), may hold values from -1.5 to 1.5
- entity_state: float32 [16384], P(('blk', 'rep')), may hold values from 0.05 to 4
- shared_table: bfloat16 [2048, 256], replicated, may hold values from -1.5 to 1.5
- shared_state: float32 [2048], P(('blk', 'rep')), may hold values from 0.05 to 4
- edge_src: int32 [8, 4, 2048], P('blk', None, 'rep'), may hold values from 0 to 2047
- edge_dst: int32 [8, 4, 2048], P('blk', None, 'rep'), may hold values from 0 to 2047
- edge_slot: int32 [8, 4, 2048], P('blk', None, 'rep'), may hold values from 0 to 63
- neg_rows: int32 [8, 4, 16, 512], P('blk', None, 'rep'), may hold values from 0 to 2047
- list_owner: int32 [8, 256, 1], P('blk', 'rep'), may hold values from 0 to 31; in each aligned block of 64 rows (0 to 63, 64 to 127, ..., all dimensions but the last counted through in order) at most 4 rows name the same one
- list_row: int32 [8, 256], P('blk', 'rep'), may hold values from 0 to 63
Outputs:
- new_entities: float32 [16384, 256], P(('blk', 'rep'))
- new_entity_state: float32 [16384], P(('blk', 'rep'))
- new_shared: float32 [2048, 256], P(('blk', 'rep'))
- new_shared_state: float32 [2048], P(('blk', 'rep'))
The draws below stay inside these ranges and needn't reach their ends.
Inputs may be any that keep to these rules, and one draw needn't show every extreme that they name: Within the 64 list entries of one device (aligned blocks of 64 entries of list_owner), no owner is named more than 4 times, a bound that some block reaches.
All inputs are finite; a program needn't handle non-finite values.
Results may differ from the reference program's by a relative error of at most 0.0022.
Values may be sent and summed in bfloat16 or wider, within the bound.
A program may use at most 64 MiB of HBM per device.

```python
import math
import jax
import jax.numpy as jnp
import numpy as np
from jax import lax

D = 256
ENT = 2048
E_DEV = 512
GROUP = 128
NEG = 512
STEPS = 4
CAP = 4
SH_DEV = 64
BLOCKS = 8
ENTITIES = 16384
EDGES = 2048
GROUPS = 16
SHARED = 2048
LIST = 64
LIST_ALL = 256
DEVICES = 32


def with_ends(values, stream_key, smallest, high):
    dims = values.shape
    index_at = [jax.random.randint(jax.random.fold_in(stream_key, axis), (), 0, dims[axis]) for axis in range(len(dims))]
    values = values.at[tuple(index_at)].set(smallest)
    longest = dims.index(max(dims))
    index_at[longest] = (index_at[longest] + 1) % dims[longest]
    return values.at[tuple(index_at)].set(high)


def block_scale(own_key, dims, pieces, smallest, largest):
    factor_of = 1.0
    for axis_at, blocks in pieces:
        heights = jax.random.uniform(jax.random.fold_in(jax.random.fold_in(own_key, 6), axis_at), (blocks,), jnp.float32, smallest / len(pieces), largest / len(pieces))
        factor_of = factor_of * jnp.repeat(jnp.exp(heights), dims[axis_at] // blocks).reshape((-1,) + (1,) * (len(dims) - 1 - axis_at))
    return factor_of


def assign_block(key, own, number, rows, amount, top, reach, skew):
    sequence = jax.random.permutation(key, amount)
    packed, common = portions_of(amount, rows * top, reach, skew, True), portions_of(amount, rows * top, reach, skew, False)
    places = jnp.arange(amount)

    def named(lengths, offset_by):
        used = int((lengths > 0).sum())
        fixed = max(1, used // 4)
        shifted = fixed + (places - fixed + offset_by * (used - fixed)) % max(1, amount - fixed)
        return jnp.zeros((amount,), jnp.int32).at[sequence[jnp.where(places < fixed, places, shifted)]].set(jnp.asarray(lengths, jnp.int32))

    lengths = jnp.where(number % 4 == 0, named(packed, number // 4), named(common, number - number // 4 - 1))
    mixed = jax.random.permutation(jax.random.fold_in(own, 3), amount)
    donor, taker = mixed[0:amount // 2 * 2:2], mixed[1:amount // 2 * 2:2]
    slack = jnp.minimum(lengths[donor] - 1, reach - lengths[taker]) // 2
    slack = jnp.where((donor == sequence[0]) | (taker == sequence[0]) | (lengths[taker] == 0), 0, jnp.maximum(slack, 0))
    shifted = jax.random.randint(jax.random.fold_in(own, 4), (amount // 2,), 0, 1 << 20) % (slack + 1)
    lengths = lengths.at[donor].add(-shifted).at[taker].add(shifted)
    items = jnp.searchsorted(jnp.cumsum(lengths), jnp.arange(rows * top), side="right").astype(jnp.int32)
    listing = items.reshape(top, rows).T
    listing = listing[jax.random.permutation(jax.random.fold_in(own, 1), rows)]
    offset_by = jax.random.randint(jax.random.fold_in(own, 2), (rows, 1), 0, top)
    return jnp.take_along_axis(listing, (jnp.arange(top)[None, :] + offset_by) % top, axis=1)


def portions_of(count, total, limit, lean, full):
    portions = [(1 << 20) // math.isqrt(standing ** lean) + 1 for standing in range(1, count + 1)]
    largest = limit if full else min(limit, max(-(-total // count), total * portions[0] // sum(portions)))
    least = 1 if total - largest >= count - 1 else 0
    given, spare = [largest] + [least] * (count - 1), total - largest - least * (count - 1)
    while spare > 0:
        free = [i for i in range(1, count) if given[i] < largest] or [i for i in range(1, count) if given[i] < limit]
        mass, budget = sum([portions[i] for i in free]), spare
        for i in free:
            more = min(limit - given[i], max(1, budget * portions[i] // mass), spare)
            given[i] = given[i] + more
            spare = spare - more
    return np.array(given)


def gaussian(own_key, extent, width, bound, shards=(), kind=jnp.bfloat16):
    factor_of = block_scale(own_key, extent, shards, -0.22, 0.18) if shards else 1.0
    result = jax.random.normal(own_key, extent, jnp.float32) * width * factor_of
    return jnp.minimum(jnp.maximum(result, -bound), bound).astype(kind)


def setup_inputs(seed: int = 0) -> dict:
    key_of = jax.random.split(jax.random.key(seed), 11)
    entities = gaussian(key_of[0], (ENTITIES, D), 0.25, 1.5, ((0, 8),))
    entity_state = jnp.clip(jnp.exp(math.log(4.0) - 4.3820266 * jax.random.uniform(key_of[1], (ENTITIES,), jnp.float32) ** block_scale(key_of[1], (ENTITIES,), ((0, 32),), -0.2, 0.2)), 0.05, 4.0)
    shared_table = gaussian(key_of[2], (SHARED, D), 0.25, 1.5)
    shared_state = jnp.clip(jnp.exp(math.log(4.0) - 4.3820266 * jax.random.uniform(key_of[3], (SHARED,), jnp.float32) ** block_scale(key_of[3], (SHARED,), ((0, 32),), -0.2, 0.2)), 0.05, 4.0)
    edge_src = with_ends(jax.random.randint(key_of[4], (BLOCKS, STEPS, EDGES), 0, ENT), jax.random.fold_in(key_of[4], 1), 0, ENT - 1).astype(jnp.int32)
    edge_dst = with_ends(jax.random.randint(key_of[5], (BLOCKS, STEPS, EDGES), 0, ENT), jax.random.fold_in(key_of[5], 1), 0, ENT - 1).astype(jnp.int32)
    edge_slot = with_ends(jax.random.randint(key_of[6], (BLOCKS, STEPS, EDGES), 0, LIST), jax.random.fold_in(key_of[6], 1), 0, LIST - 1).astype(jnp.int32)
    neg_rows = with_ends(jax.random.randint(key_of[7], (BLOCKS, STEPS, GROUPS, NEG), 0, ENT), jax.random.fold_in(key_of[7], 1), 0, ENT - 1).astype(jnp.int32)
    list_owner_keys = jax.random.split(jax.random.fold_in(key_of[8], 1), BLOCKS * LIST_ALL // LIST)
    list_owner_turns = jax.random.permutation(jax.random.fold_in(key_of[8], 3), BLOCKS * LIST_ALL // LIST)
    list_owner = jax.vmap(lambda own, number: assign_block(jax.random.fold_in(key_of[8], 2), own, number, LIST, DEVICES, 1, CAP, 2))(list_owner_keys, list_owner_turns).reshape((BLOCKS, LIST_ALL, 1))
    list_row = with_ends(jax.random.randint(key_of[9], (BLOCKS, LIST_ALL), 0, SH_DEV), jax.random.fold_in(key_of[9], 1), 0, SH_DEV - 1).astype(jnp.int32)
    return {"entities": entities, "entity_state": entity_state, "shared_table": shared_table, "shared_state": shared_state, "edge_src": edge_src, "edge_dst": edge_dst, "edge_slot": edge_slot, "neg_rows": neg_rows, "list_owner": list_owner, "list_row": list_row}


learn_rate = 0.1
negative_weight = 8.0

def row_adagrad(rows, state, grad):
    new_state = state + lax.optimization_barrier(jnp.mean(grad * grad, axis=-1))
    return (rows.astype(jnp.float32) - learn_rate * grad / jnp.sqrt(new_state)[:, None], new_state)

def reference(entities, entity_state, shared_table, shared_state, edge_src, edge_dst, edge_slot, neg_rows, list_owner, list_row):
    shared_ids = list_owner[:, :, 0] * SH_DEV + list_row
    list_base = jnp.arange(EDGES, dtype=jnp.int32) // E_DEV * LIST

    def visit(carry, bucket_index):
        entity_grad, shared_grad = carry
        source_part = bucket_index // STEPS
        bucket = bucket_index % STEPS
        target_part = (source_part - bucket) % BLOCKS
        sources = edge_src[source_part, bucket] + source_part * ENT
        targets = edge_dst[source_part, bucket] + target_part * ENT
        slots = shared_ids[source_part][edge_slot[source_part, bucket] + list_base]
        negatives = neg_rows[source_part, bucket] + target_part * ENT
        query = (entities[sources].astype(jnp.float32) + shared_table[slots].astype(jnp.float32)).astype(jnp.bfloat16)
        query = lax.optimization_barrier(query)
        query_wide = query.astype(jnp.float32)
        target_rows = entities[targets].astype(jnp.float32)
        positive = lax.optimization_barrier(jnp.sum(query_wide * target_rows, axis=-1))
        samples = entities[negatives].astype(jnp.float32)
        query_groups = query_wide.reshape(GROUPS, GROUP, D)
        negative = jnp.einsum('cqd,cnd->cqn', query_groups, samples)
        positive_weight = -jax.nn.sigmoid(-positive)
        sample_weight = (jax.nn.sigmoid(negative) * (negative_weight / NEG)).astype(jnp.bfloat16)
        sample_weight = lax.optimization_barrier(sample_weight).astype(jnp.float32)
        query_grad = positive_weight[:, None] * target_rows + jnp.einsum('cqn,cnd->cqd', sample_weight, samples).reshape(EDGES, D)
        target_grad = positive_weight[:, None] * query_wide
        sample_grad = jnp.einsum('cqn,cqd->cnd', sample_weight, query_groups).reshape(GROUPS * NEG, D)
        entity_grad = entity_grad.at[sources].add(query_grad).at[targets].add(target_grad).at[negatives.reshape(-1)].add(sample_grad)
        shared_grad = shared_grad.at[slots].add(query_grad)
        return ((entity_grad, shared_grad), None)
    start = (jnp.zeros((ENTITIES, D), jnp.float32), jnp.zeros((SHARED, D), jnp.float32))
    (entity_grad, shared_grad), unused = lax.scan(visit, start, jnp.arange(BLOCKS * STEPS, dtype=jnp.int32))
    new_entities, new_entity_state = row_adagrad(entities, entity_state, entity_grad)
    new_shared, new_shared_state = row_adagrad(shared_table, shared_state, shared_grad)
    return (new_entities, new_entity_state, new_shared, new_shared_state)
```

```python
import jax
import jax.numpy as jnp
from jax import lax
from jax.sharding import PartitionSpec as P

CAP = 4
SH_DEV = 64
LANES = 128


learn_rate = 0.1
negative_weight = 8.0


def passed_along(value, axis, by):
    peers = lax.axis_size(axis)
    return lax.ppermute(value, axis, [(i, (i + by) % peers) for i in range(peers)])


def one_hot(ids, count, dtype=jnp.bfloat16):
    return (ids[..., None] == jnp.arange(count, dtype=jnp.int32)).astype(dtype)


def row_counts(negatives, part_rows):
    high = one_hot(negatives // LANES, part_rows // LANES)
    low = one_hot(negatives % LANES, LANES)
    counts = jnp.einsum("cnh,cnl->chl", high, low, preferred_element_type=jnp.float32)
    return counts.reshape(negatives.shape[0], part_rows)


def scatter_rows(pick, rows):
    return lax.dot_general(
        pick, rows, (((0,), (0,)), ((), ())), preferred_element_type=jnp.float32
    )


def bucket_grads(resident, query, targets, negatives):
    part_rows = resident.shape[0]
    edges = query.shape[0]
    group_count, sample_count = negatives.shape
    counts = row_counts(negatives, part_rows) * (negative_weight / sample_count)
    counts = jnp.repeat(counts, edges // group_count, axis=0)
    scores = lax.dot_general(
        query, resident, (((1,), (1,)), ((), ())), preferred_element_type=jnp.float32
    )
    sigmoid = 0.5 * jnp.tanh(0.5 * scores) + 0.5
    target = one_hot(targets, part_rows, jnp.float32)
    weight = (sigmoid * (counts + target) - target).astype(jnp.bfloat16)
    query_grad = jnp.dot(weight, resident, preferred_element_type=jnp.float32)
    return query_grad.astype(jnp.bfloat16), scatter_rows(weight, query)


def row_adagrad(rows, state, grad):
    new_state = state + jnp.mean(grad * grad, axis=-1)
    return (rows.astype(jnp.float32) - learn_rate * grad / jnp.sqrt(new_state)[:, None], new_state)


def shards(
    entities,
    entity_state,
    shared_table,
    shared_state,
    edge_src,
    edge_dst,
    edge_slot,
    neg_rows,
    list_owner,
    list_row,
):
    rep_count = lax.axis_size("rep")
    rep_place = lax.axis_index("rep")
    device_count = lax.axis_size("blk") * rep_count
    device_place = lax.axis_index("blk") * rep_count + rep_place
    part_rows, model_width = entities.shape
    share_rows = part_rows // rep_count
    bucket_count, edges = edge_src.shape[1:]
    group_count, sample_count = neg_rows.shape[2:]
    owners = list_owner[0, :, 0]
    local_rows = list_row[0]
    slot_count = owners.shape[0]
    ids = []
    for bucket in range(bucket_count):
        own = jnp.concatenate([edge_dst[0, bucket], neg_rows[0, bucket].reshape(-1)])
        ids.append(passed_along(own, "blk", -bucket) if bucket else own)
    shared_rows = shared_table[owners * SH_DEV + local_rows]
    source_picks = [one_hot(edge_src[0, b], part_rows) for b in range(bucket_count)]
    slot_picks = [one_hot(edge_slot[0, b], slot_count) for b in range(bucket_count)]
    queries = []
    for bucket in range(bucket_count):
        source_rows = jnp.dot(source_picks[bucket], entities, preferred_element_type=jnp.float32)
        shared_part = jnp.dot(slot_picks[bucket], shared_rows, preferred_element_type=jnp.float32)
        query = (source_rows + shared_part).astype(jnp.bfloat16)
        queries.append(passed_along(query, "blk", -bucket) if bucket else query)
    grad = jnp.zeros((part_rows, model_width), jnp.float32)
    query_grads = []
    for bucket in range(bucket_count):
        query_grad, target_grad = bucket_grads(
            entities,
            queries[bucket],
            ids[bucket][:edges],
            ids[bucket][edges:].reshape(group_count, sample_count),
        )
        grad = grad + target_grad
        query_grads.append(passed_along(query_grad, "blk", bucket) if bucket else query_grad)
    slot_total = jnp.zeros((slot_count, model_width), jnp.float32)
    for bucket in range(bucket_count):
        grad = grad + scatter_rows(source_picks[bucket], query_grads[bucket])
        slot_total = slot_total + scatter_rows(slot_picks[bucket], query_grads[bucket])
    slot_order = jnp.arange(slot_count, dtype=jnp.int32)
    earlier_same = (owners[:, None] == owners[None, :]) & (
        slot_order[None, :] < slot_order[:, None]
    )
    slot_ranks = jnp.sum(earlier_same.astype(jnp.int32), axis=1)
    send_pick = one_hot(owners * CAP + slot_ranks, device_count * CAP)
    outbound = scatter_rows(send_pick, slot_total.astype(jnp.bfloat16)).astype(jnp.bfloat16)
    labels = scatter_rows(send_pick, local_rows.astype(jnp.bfloat16)[:, None]).astype(jnp.bfloat16)
    outbound = jnp.concatenate(
        [
            outbound.reshape(device_count, CAP * model_width),
            jnp.pad(labels.reshape(device_count, CAP), ((0, 0), (0, LANES - CAP))),
        ],
        axis=1,
    )
    inbound = lax.all_to_all(outbound, ("blk", "rep"), split_axis=0, concat_axis=0, tiled=True)
    own_grad = lax.psum_scatter(
        grad.astype(jnp.bfloat16), "rep", scatter_dimension=0, tiled=True
    ).astype(jnp.float32)
    own_entities = lax.dynamic_slice_in_dim(entities, rep_place * share_rows, share_rows, 0)
    new_entities, new_entity_state = row_adagrad(own_entities, entity_state, own_grad)
    in_rows = inbound[:, : CAP * model_width].reshape(device_count * CAP, model_width)
    in_labels = inbound[:, CAP * model_width : CAP * model_width + CAP].reshape(-1)
    shared_grad = scatter_rows(one_hot(in_labels.astype(jnp.int32), SH_DEV), in_rows)
    own_shared = lax.dynamic_slice_in_dim(shared_table, device_place * SH_DEV, SH_DEV, 0)
    new_shared, new_shared_state = row_adagrad(own_shared, shared_state, shared_grad)
    return (new_entities, new_entity_state, new_shared, new_shared_state)


def solution(mesh):
    return jax.shard_map(
        shards,
        mesh=mesh,
        in_specs=(
            P("blk", None),
            P(("blk", "rep")),
            P(),
            P(("blk", "rep")),
            P("blk", None, "rep"),
            P("blk", None, "rep"),
            P("blk", None, "rep"),
            P("blk", None, "rep", None),
            P("blk", "rep", None),
            P("blk", "rep"),
        ),
        out_specs=(
            P(("blk", "rep"), None),
            P(("blk", "rep")),
            P(("blk", "rep"), None),
            P(("blk", "rep")),
        ),
        check_vma=False,
    )
```

```python
import functools

import jax
import jax.numpy as jnp
from jax import lax
from jax.experimental import pallas as pl
from jax.experimental.pallas import tpu as pltpu
from jax.sharding import PartitionSpec as P

CAP = 4
SH_DEV = 64
LANES = 128
CHUNK = 512
SLAB = 8


learn_rate = 0.1
negative_weight = 8.0
MESH = pl.DeviceIdType.MESH
f32 = jnp.float32
bf16 = jnp.bfloat16


def dot(a, b):
    return jnp.dot(a, b, preferred_element_type=f32)


def dot_split(a, b):
    high = b.astype(bf16)
    low = (b - high.astype(f32)).astype(bf16)
    return dot(a, high) + dot(a, low)


def columns(row):
    return jnp.transpose(jnp.broadcast_to(row.astype(f32), (LANES, row.shape[1])))


def tiled(cols, width):
    return jnp.concatenate([cols] * (width // LANES), axis=1)


def lane_hot(cols, start, width):
    ids = lax.broadcasted_iota(jnp.int32, (cols.shape[0], width), 1) + start
    return tiled(cols, width) == ids.astype(f32)


def kernel(
    groups,
    ent_ref,
    table_ref,
    ids_ref,
    list_ref,
    ent_state_ref,
    sh_state_ref,
    new_ent_ref,
    new_ent_state_ref,
    new_sh_ref,
    new_sh_state_ref,
    vt_ref,
    pick_ref,
    slot_ref,
    q_out,
    q_in,
    ids_in,
    qg_out,
    qg_in,
    dcol_ref,
    cnt_ref,
    qg_ref,
    gt_ref,
    rs_out,
    rs_in,
    sh_out,
    sh_in,
    q_send,
    q_recv,
    i_send,
    i_recv,
    g_send,
    g_recv,
    r_send,
    r_recv,
    s_send,
    s_recv,
):
    blk, rep = lax.axis_index("blk"), lax.axis_index("rep")
    blks, reps = lax.axis_size("blk"), lax.axis_size("rep")
    devices = blks * reps
    me = blk * reps + rep
    rows, width = ent_ref.shape
    buckets, edges = ids_ref.shape[0], ids_ref.shape[2]
    group_edges = edges // groups
    chunks = rows // CHUNK
    highs = rows // LANES
    share = rows // reps
    list_pad = list_ref.shape[1]

    def place(peer):
        return (peer // reps, lax.rem(peer, reps))

    barrier = pltpu.get_barrier_semaphore()

    def greet(off, _):
        pl.semaphore_signal(
            barrier,
            inc=1,
            device_id=place(lax.rem(me + off, devices)),
            device_id_type=MESH,
        )
        return 0

    lax.fori_loop(1, devices, greet, 0)

    vt_ref[...] = jnp.transpose(ent_ref[...].astype(f32)).astype(bf16)
    id_cols = columns(list_ref[0:1, :])
    shared_rows = jnp.zeros((list_pad, width), f32)
    step = min(2048, table_ref.shape[0])
    for start in range(0, table_ref.shape[0], step):
        hot = jnp.where(lane_hot(id_cols, start, step), 1.0, 0.0).astype(bf16)
        shared_rows = shared_rows + dot(hot, table_ref[start : start + step, :])
    shared_rows = shared_rows.astype(bf16)

    def to_back(bucket):
        return (lax.rem(blk - bucket + blks, blks), rep)

    def to_front(bucket):
        return (lax.rem(blk + bucket, blks), rep)

    def id_copy(bucket):
        return pltpu.make_async_remote_copy(
            src_ref=ids_ref.at[bucket],
            dst_ref=ids_in.at[bucket],
            send_sem=i_send.at[bucket],
            recv_sem=i_recv.at[bucket],
            device_id=to_back(bucket),
            device_id_type=MESH,
        )

    def query_copy(bucket):
        return pltpu.make_async_remote_copy(
            src_ref=q_out.at[bucket],
            dst_ref=q_in.at[bucket],
            send_sem=q_send.at[bucket],
            recv_sem=q_recv.at[bucket],
            device_id=to_back(bucket),
            device_id_type=MESH,
        )

    def grad_copy(bucket):
        return pltpu.make_async_remote_copy(
            src_ref=qg_out.at[bucket],
            dst_ref=qg_in.at[bucket],
            send_sem=g_send.at[bucket],
            recv_sem=g_recv.at[bucket],
            device_id=to_front(bucket),
            device_id_type=MESH,
        )

    def make_query(bucket):
        slot = jnp.where(lane_hot(columns(ids_ref[bucket, 6:7, :]), 0, list_pad), 1.0, 0.0)
        slot_ref[bucket] = slot.astype(bf16)
        dcol_ref[...] = columns(ids_ref[bucket, 5:6, :])
        qg_ref[...] = dot(slot_ref[bucket], shared_rows)

        def body(c, _):
            at = pl.multiple_of(c * CHUNK, CHUNK)
            pick = jnp.where(lane_hot(dcol_ref[...], at, CHUNK), 1.0, 0.0).astype(bf16)
            pick_ref[bucket, :, pl.ds(at, CHUNK)] = pick
            qg_ref[...] += dot(pick, ent_ref[pl.ds(at, CHUNK), :])
            return 0

        lax.fori_loop(0, chunks, body, 0)
        q_out[bucket] = qg_ref[...].astype(bf16)

    def score(query_ref, id_ref, out_ref, first):
        query = query_ref[...]
        query_t = jnp.transpose(query.astype(f32)).astype(bf16)
        dcol_ref[...] = columns(id_ref[0:1, :])
        for g in range(groups):
            ids = id_ref[1 + g : 2 + g, :]
            high = lax.broadcasted_iota(jnp.int32, (highs, ids.shape[1]), 0) == ids // LANES
            low = lax.broadcasted_iota(jnp.int32, (LANES, ids.shape[1]), 0) == lax.rem(ids, LANES)
            counts = lax.dot_general(
                jnp.where(high, 1.0, 0.0).astype(bf16),
                jnp.where(low, 1.0, 0.0).astype(bf16),
                (((1,), (1,)), ((), ())),
                preferred_element_type=f32,
            )
            cnt_ref[g * highs : (g + 1) * highs, :] = counts * (negative_weight / ids.shape[1])
        qg_ref[...] = jnp.zeros_like(qg_ref)

        def body(c, _):
            at = pl.multiple_of(c * CHUNK, CHUNK)
            scores = dot(query, vt_ref[:, pl.ds(at, CHUNK)])
            sigmoid = 0.5 * jnp.tanh(0.5 * scores) + 0.5
            per = CHUNK // LANES
            counts = jnp.concatenate(
                [
                    jnp.concatenate(
                        [
                            jnp.broadcast_to(
                                cnt_ref[pl.ds(g * highs + c * per + h, 1), :],
                                (group_edges, LANES),
                            )
                            for h in range(per)
                        ],
                        axis=1,
                    )
                    for g in range(groups)
                ],
                axis=0,
            )
            target = lane_hot(dcol_ref[...], at, CHUNK)
            sampled = sigmoid * counts
            weight = jnp.where(target, sampled + sigmoid - 1.0, sampled).astype(bf16)
            qg_ref[...] += dot(weight, ent_ref[pl.ds(at, CHUNK), :])
            grown = dot(query_t, weight)
            if first:
                gt_ref[:, pl.ds(at, CHUNK)] = grown
            else:
                gt_ref[:, pl.ds(at, CHUNK)] += grown
            return 0

        lax.fori_loop(0, chunks, body, 0)
        out_ref[...] = jnp.transpose(qg_ref[...]).astype(bf16)

    make_query(1)
    pl.semaphore_wait(barrier, devices - 1)
    for bucket in range(1, buckets):
        id_copy(bucket).start()
    for bucket in range(1, buckets):
        if bucket > 1:
            make_query(bucket)
        query_copy(bucket).start()
    make_query(0)
    score(q_out.at[0], ids_ref.at[0], qg_out.at[0], True)
    for bucket in range(1, buckets):
        id_copy(bucket).wait_recv()
        query_copy(bucket).wait_recv()
        score(q_in.at[bucket], ids_in.at[bucket], qg_out.at[bucket], False)
        grad_copy(bucket).start()

    slot_total = jnp.zeros((width, list_pad), f32)
    for bucket in range(buckets):
        if bucket:
            grad_copy(bucket).wait_recv()
            back = qg_in[bucket]
        else:
            back = qg_out[0]
        slot_total = slot_total + dot(back, slot_ref[bucket])

        def body(c, _, back=back, bucket=bucket):
            at = pl.ds(pl.multiple_of(c * CHUNK, CHUNK), CHUNK)
            gt_ref[:, at] += dot(back, pick_ref[bucket, :, at])
            return 0

        lax.fori_loop(0, chunks, body, 0)

    def share_copy(peer):
        return pltpu.make_async_remote_copy(
            src_ref=rs_out.at[peer],
            dst_ref=rs_in.at[rep],
            send_sem=r_send.at[peer],
            recv_sem=r_recv.at[rep],
            device_id=(blk, peer),
            device_id_type=MESH,
        )

    for off in range(1, reps):
        peer = lax.rem(rep + off, reps)
        at = pl.ds(pl.multiple_of(peer * share, share), share)
        rs_out[peer] = gt_ref[:, at].astype(bf16)
        share_copy(peer).start()

    keys = list_ref[1:2, :]
    hot = lax.broadcasted_iota(jnp.int32, (devices * SLAB, list_pad), 0) == keys
    sh_out[:, :width] = dot_split(
        jnp.where(hot, 1.0, 0.0).astype(bf16), jnp.transpose(slot_total)
    )
    marks = jnp.where(hot, list_ref[2:3, :].astype(f32), 0.0).astype(bf16)
    sh_out[:, width:] = dot(marks, jnp.ones((list_pad, LANES), bf16))

    def slab(ref, peer):
        return ref.at[pl.ds(pl.multiple_of(peer * SLAB, SLAB), SLAB), :]

    def slab_copy(peer):
        return pltpu.make_async_remote_copy(
            src_ref=slab(sh_out, peer),
            dst_ref=slab(sh_in, me),
            send_sem=s_send.at[peer],
            recv_sem=s_recv.at[me],
            device_id=place(peer),
            device_id_type=MESH,
        )

    def slab_start(off, _):
        slab_copy(lax.rem(me + off, devices)).start()
        return 0

    lax.fori_loop(1, devices, slab_start, 0)
    own = pl.ds(pl.multiple_of(me * SLAB, SLAB), SLAB)
    sh_in[own, :] = sh_out[own, :]

    def slab_wait(off, _):
        peer = lax.rem(me + off, devices)
        pltpu.make_async_remote_copy(
            src_ref=slab(sh_out, peer),
            dst_ref=slab(sh_in, peer),
            send_sem=s_send.at[peer],
            recv_sem=s_recv.at[peer],
            device_id=place(peer),
            device_id_type=MESH,
        ).wait()
        return 0

    lax.fori_loop(1, devices, slab_wait, 0)
    labels = jnp.transpose(sh_in[:, width:])[:SH_DEV, :]
    hot = labels == lax.broadcasted_iota(jnp.int32, labels.shape, 0).astype(f32)
    shared_grad = dot_split(jnp.where(hot, 1.0, 0.0).astype(bf16), sh_in[:, :width])
    new_state = sh_state_ref[...] + jnp.mean(shared_grad * shared_grad, axis=1, keepdims=True)
    new_sh_state_ref[...] = new_state
    own_shared = table_ref[pl.ds(pl.multiple_of(me * SH_DEV, SH_DEV), SH_DEV), :].astype(f32)
    new_sh_ref[...] = own_shared - learn_rate * shared_grad / jnp.sqrt(new_state)

    own = pl.ds(pl.multiple_of(rep * share, share), share)
    grad = gt_ref[:, own]
    for off in range(1, reps):
        peer = lax.rem(rep + reps - off, reps)
        pltpu.make_async_remote_copy(
            src_ref=rs_out.at[peer],
            dst_ref=rs_in.at[peer],
            send_sem=r_send.at[peer],
            recv_sem=r_recv.at[peer],
            device_id=(blk, peer),
            device_id_type=MESH,
        ).wait()
        grad = grad + rs_in[peer].astype(f32)
    new_state = ent_state_ref[...] + jnp.mean(grad * grad, axis=0, keepdims=True)
    new_ent_state_ref[...] = new_state
    update = jnp.transpose(learn_rate * grad / jnp.sqrt(new_state))
    new_ent_ref[...] = ent_ref[own, :].astype(f32) - update
    for bucket in range(1, buckets):
        id_copy(bucket).wait_send()
        query_copy(bucket).wait_send()
        grad_copy(bucket).wait_send()


def shards(
    entities,
    entity_state,
    shared_table,
    shared_state,
    edge_src,
    edge_dst,
    edge_slot,
    neg_rows,
    list_owner,
    list_row,
):
    reps = lax.axis_size("rep")
    devices = lax.axis_size("blk") * reps
    rows, width = entities.shape
    share = rows // reps
    buckets, edges = edge_src.shape[1:]
    groups = neg_rows.shape[2]
    owners = list_owner[0, :, 0]
    count = owners.shape[0]
    list_pad = -(-count // LANES) * LANES
    order = jnp.arange(count, dtype=jnp.int32)
    earlier = (owners[:, None] == owners[None, :]) & (order[:, None] < order[None, :])
    ranks = jnp.sum(earlier.astype(jnp.int32), axis=0)
    lists = jnp.stack([owners * SH_DEV + list_row[0], owners * SLAB + ranks, list_row[0]])
    lists = jnp.pad(lists, ((0, 5), (0, list_pad - count)), constant_values=-1)
    ids = jnp.concatenate(
        [
            edge_dst[0][:, None],
            neg_rows[0],
            edge_src[0][:, None],
            edge_slot[0][:, None],
            jnp.zeros((buckets, 1, edges), jnp.int32),
        ],
        axis=1,
    )
    sems = pltpu.SemaphoreType.DMA
    vmem = pl.BlockSpec(memory_space=pltpu.VMEM)
    new_entities, new_entity_state, new_shared, new_shared_state = pl.pallas_call(
        functools.partial(kernel, groups),
        out_shape=(
            jax.ShapeDtypeStruct((share, width), f32),
            jax.ShapeDtypeStruct((1, share), f32),
            jax.ShapeDtypeStruct((SH_DEV, width), f32),
            jax.ShapeDtypeStruct((SH_DEV, 1), f32),
        ),
        in_specs=[vmem] * 6,
        out_specs=[vmem] * 4,
        scratch_shapes=[
            pltpu.VMEM((width, rows), bf16),
            pltpu.VMEM((buckets, edges, rows), bf16),
            pltpu.VMEM((buckets, edges, list_pad), bf16),
            pltpu.VMEM((buckets, edges, width), bf16),
            pltpu.VMEM((buckets, edges, width), bf16),
            pltpu.VMEM((buckets, 8, edges), jnp.int32),
            pltpu.VMEM((buckets, width, edges), bf16),
            pltpu.VMEM((buckets, width, edges), bf16),
            pltpu.VMEM((edges, LANES), f32),
            pltpu.VMEM((groups * (rows // LANES), LANES), f32),
            pltpu.VMEM((edges, width), f32),
            pltpu.VMEM((width, rows), f32),
            pltpu.VMEM((reps, width, share), bf16),
            pltpu.VMEM((reps, width, share), bf16),
            pltpu.VMEM((devices * SLAB, width + LANES), f32),
            pltpu.VMEM((devices * SLAB, width + LANES), f32),
            sems((buckets,)),
            sems((buckets,)),
            sems((buckets,)),
            sems((buckets,)),
            sems((buckets,)),
            sems((buckets,)),
            sems((reps,)),
            sems((reps,)),
            sems((devices,)),
            sems((devices,)),
        ],
        compiler_params=pltpu.CompilerParams(
            collective_id=0, has_side_effects=True, vmem_limit_bytes=56 * 2**20
        ),
    )(
        entities,
        shared_table,
        ids,
        lists,
        entity_state.reshape(1, share),
        shared_state.reshape(SH_DEV, 1),
    )
    return (
        new_entities,
        new_entity_state.reshape(share),
        new_shared,
        new_shared_state.reshape(SH_DEV),
    )


def solution(mesh):
    return jax.shard_map(
        shards,
        mesh=mesh,
        in_specs=(
            P("blk", None),
            P(("blk", "rep")),
            P(),
            P(("blk", "rep")),
            P("blk", None, "rep"),
            P("blk", None, "rep"),
            P("blk", None, "rep"),
            P("blk", None, "rep", None),
            P("blk", "rep", None),
            P("blk", "rep"),
        ),
        out_specs=(
            P(("blk", "rep"), None),
            P(("blk", "rep")),
            P(("blk", "rep"), None),
            P(("blk", "rep")),
        ),
        check_vma=False,
    )
```

```python
import functools

import jax
import jax.numpy as jnp
from jax import lax
from jax.experimental import pallas as pl
from jax.experimental.pallas import tpu as pltpu
from jax.sharding import PartitionSpec as P

CAP = 4
SH_DEV = 64
LANES = 128
CHUNK = 512
SLAB = 16


learn_rate = 0.1
negative_weight = 8.0
MESH = pl.DeviceIdType.MESH
f32 = jnp.float32
bf16 = jnp.bfloat16


def dot(a, b):
    return jnp.dot(a, b, preferred_element_type=f32)


def columns(row):
    return jnp.transpose(jnp.broadcast_to(row.astype(f32), (LANES, row.shape[1])))


def tiled(cols, width):
    return jnp.concatenate([cols] * (width // LANES), axis=1)


def lane_hot(cols, start, width):
    ids = lax.broadcasted_iota(jnp.int32, (cols.shape[0], width), 1) + start
    return tiled(cols, width) == ids.astype(f32)


def kernel(
    groups,
    ent_ref,
    table_ref,
    src_ref,
    dst_ref,
    slots_ref,
    neg_ref,
    owner_ref,
    row_ref,
    ent_state_ref,
    sh_state_ref,
    new_ent_ref,
    new_ent_state_ref,
    new_sh_ref,
    new_sh_state_ref,
    ids_ref,
    list_ref,
    vt_ref,
    pick_ref,
    slot_ref,
    q_out,
    q_in,
    ids_in,
    qg_out,
    qg_in,
    dcol_ref,
    cnt_ref,
    qg_ref,
    gt_ref,
    rs_out,
    rs_in,
    sh_out,
    sh_in,
    q_send,
    q_recv,
    i_send,
    i_recv,
    g_send,
    g_recv,
    r_send,
    r_recv,
    s_send,
    s_recv,
):
    blk, rep = lax.axis_index("blk"), lax.axis_index("rep")
    blks, reps = lax.axis_size("blk"), lax.axis_size("rep")
    devices = blks * reps
    me = blk * reps + rep
    rows, width = ent_ref.shape
    buckets, edges = src_ref.shape[1:]
    group_edges = edges // groups
    chunks = rows // CHUNK
    highs = rows // LANES
    share = rows // reps
    list_pad = list_ref.shape[1]

    def place(peer):
        return (peer // reps, lax.rem(peer, reps))

    barrier = pltpu.get_barrier_semaphore()

    def greet(off, _):
        pl.semaphore_signal(
            barrier,
            inc=1,
            device_id=place(lax.rem(me + off, devices)),
            device_id_type=MESH,
        )
        return 0

    lax.fori_loop(1, devices, greet, 0)

    for bucket in range(buckets):
        ids_ref[bucket, 0:1, :] = dst_ref[0, bucket : bucket + 1, :]
        ids_ref[bucket, 1 : 1 + groups, :] = neg_ref[0, bucket]
        ids_ref[bucket, 1 + groups : 2 + groups, :] = src_ref[0, bucket : bucket + 1, :]
        ids_ref[bucket, 2 + groups : 3 + groups, :] = slots_ref[0, bucket : bucket + 1, :]
        ids_ref[bucket, 3 + groups :, :] = jnp.zeros((8 - 3 - groups, edges), jnp.int32)
    count = row_ref.shape[1]
    owner_cols = jnp.broadcast_to(owner_ref[0].astype(f32), (count, LANES))
    owners = jnp.transpose(owner_cols)[0:1, :]
    same = jnp.broadcast_to(owner_ref[0].astype(f32), (count, count)) == owners
    earlier = lax.broadcasted_iota(jnp.int32, (count, count), 0) < lax.broadcasted_iota(
        jnp.int32, (count, count), 1
    )
    ranks = jnp.sum(jnp.where(same & earlier, 1.0, 0.0), axis=0, keepdims=True)
    owners = owners.astype(jnp.int32)
    list_ref[...] = jnp.full(list_ref.shape, -SH_DEV, jnp.int32)
    list_ref[0:1, :count] = owners * SH_DEV + row_ref[...]
    list_ref[1:2, :count] = owners * SLAB + ranks.astype(jnp.int32)
    list_ref[2:3, :count] = row_ref[...]

    vt_ref[...] = jnp.transpose(ent_ref[...].astype(f32)).astype(bf16)
    id_cols = columns(list_ref[0:1, :])
    shared_rows = jnp.zeros((list_pad, width), f32)
    step = min(2048, table_ref.shape[0])
    for start in range(0, table_ref.shape[0], step):
        hot = jnp.where(lane_hot(id_cols, start, step), 1.0, 0.0).astype(bf16)
        shared_rows = shared_rows + dot(hot, table_ref[start : start + step, :])
    shared_rows = shared_rows.astype(bf16)

    def to_back(bucket):
        return (lax.rem(blk - bucket + blks, blks), rep)

    def to_front(bucket):
        return (lax.rem(blk + bucket, blks), rep)

    def id_copy(bucket):
        return pltpu.make_async_remote_copy(
            src_ref=ids_ref.at[bucket],
            dst_ref=ids_in.at[bucket],
            send_sem=i_send.at[bucket],
            recv_sem=i_recv.at[bucket],
            device_id=to_back(bucket),
            device_id_type=MESH,
        )

    def query_copy(bucket):
        return pltpu.make_async_remote_copy(
            src_ref=q_out.at[bucket],
            dst_ref=q_in.at[bucket],
            send_sem=q_send.at[bucket],
            recv_sem=q_recv.at[bucket],
            device_id=to_back(bucket),
            device_id_type=MESH,
        )

    def grad_copy(bucket):
        return pltpu.make_async_remote_copy(
            src_ref=qg_out.at[bucket],
            dst_ref=qg_in.at[bucket],
            send_sem=g_send.at[bucket],
            recv_sem=g_recv.at[bucket],
            device_id=to_front(bucket),
            device_id_type=MESH,
        )

    def make_query(bucket):
        slot = jnp.where(lane_hot(columns(ids_ref[bucket, 2 + groups : 3 + groups, :]), 0, list_pad), 1.0, 0.0)
        slot_ref[bucket] = slot.astype(bf16)
        dcol_ref[...] = columns(ids_ref[bucket, 1 + groups : 2 + groups, :])
        qg_ref[...] = dot(slot_ref[bucket], shared_rows)

        def body(c, _):
            at = pl.multiple_of(c * CHUNK, CHUNK)
            pick = jnp.where(lane_hot(dcol_ref[...], at, CHUNK), 1.0, 0.0).astype(bf16)
            pick_ref[bucket * edges : (bucket + 1) * edges, pl.ds(at, CHUNK)] = pick
            qg_ref[...] += dot(pick, ent_ref[pl.ds(at, CHUNK), :])
            return 0

        lax.fori_loop(0, chunks, body, 0, unroll=True)
        q_out[bucket] = qg_ref[...].astype(bf16)

    def score(query_ref, id_ref, out_ref, first):
        query = query_ref[...]
        query_t = jnp.transpose(query.astype(f32)).astype(bf16)
        dcol_ref[...] = columns(id_ref[0:1, :])
        for g in range(groups):
            ids = id_ref[1 + g : 2 + g, :]
            high = lax.broadcasted_iota(jnp.int32, (highs, ids.shape[1]), 0) == ids // LANES
            low = lax.broadcasted_iota(jnp.int32, (LANES, ids.shape[1]), 0) == lax.rem(ids, LANES)
            counts = lax.dot_general(
                jnp.where(high, 1.0, 0.0).astype(bf16),
                jnp.where(low, 1.0, 0.0).astype(bf16),
                (((1,), (1,)), ((), ())),
                preferred_element_type=f32,
            )
            cnt_ref[g * highs : (g + 1) * highs, :] = counts * (negative_weight / ids.shape[1])
        qg_ref[...] = jnp.zeros_like(qg_ref)

        def body(c, _):
            at = pl.multiple_of(c * CHUNK, CHUNK)
            scores = dot(query, vt_ref[:, pl.ds(at, CHUNK)])
            sigmoid = 0.5 * jnp.tanh(0.5 * scores) + 0.5
            per = CHUNK // LANES
            counts = jnp.concatenate(
                [
                    jnp.concatenate(
                        [
                            jnp.broadcast_to(
                                cnt_ref[pl.ds(g * highs + c * per + h, 1), :],
                                (group_edges, LANES),
                            )
                            for h in range(per)
                        ],
                        axis=1,
                    )
                    for g in range(groups)
                ],
                axis=0,
            )
            target = lane_hot(dcol_ref[...], at, CHUNK)
            sampled = sigmoid * counts
            weight = jnp.where(target, sampled + sigmoid - 1.0, sampled).astype(bf16)
            qg_ref[...] += dot(weight, ent_ref[pl.ds(at, CHUNK), :])
            grown = dot(query_t, weight)
            if first:
                gt_ref[:, pl.ds(at, CHUNK)] = grown
            else:
                gt_ref[:, pl.ds(at, CHUNK)] += grown
            return 0

        lax.fori_loop(0, chunks, body, 0, unroll=True)
        out_ref[...] = jnp.transpose(qg_ref[...]).astype(bf16)

    make_query(1)
    pl.semaphore_wait(barrier, devices - 1)
    for bucket in range(1, buckets):
        id_copy(bucket).start()
    for bucket in range(1, buckets):
        if bucket > 1:
            make_query(bucket)
        query_copy(bucket).start()
    make_query(0)
    score(q_out.at[0], ids_ref.at[0], qg_out.at[0], True)
    for bucket in range(1, buckets):
        id_copy(bucket).wait_recv()
        query_copy(bucket).wait_recv()
        score(q_in.at[bucket], ids_in.at[bucket], qg_out.at[bucket], False)
        grad_copy(bucket).start()

    for bucket in range(1, buckets):
        grad_copy(bucket).wait_recv()
    backs = [qg_out[0]] + [qg_in[bucket] for bucket in range(1, buckets)]
    backs = jnp.concatenate(backs, axis=1)

    def share_grad(peer):
        at = pl.ds(pl.multiple_of(peer * share, share), share)
        return gt_ref[:, at] + dot(backs, pick_ref[:, at])

    def share_copy(peer):
        return pltpu.make_async_remote_copy(
            src_ref=rs_out.at[peer],
            dst_ref=rs_in.at[rep],
            send_sem=r_send.at[peer],
            recv_sem=r_recv.at[rep],
            device_id=(blk, peer),
            device_id_type=MESH,
        )

    for off in range(1, reps):
        peer = lax.rem(rep + off, reps)
        rs_out[peer] = share_grad(peer).astype(bf16)
        share_copy(peer).start()

    slot_total = jnp.zeros((width, list_pad), f32)
    for bucket in range(buckets):
        back = backs[:, bucket * edges : (bucket + 1) * edges]
        slot_total = slot_total + dot(back, slot_ref[bucket])
    slot_total = jnp.transpose(slot_total).astype(bf16)
    places = lax.broadcasted_iota(jnp.int32, (devices * SLAB, list_pad), 0)
    keys = list_ref[1:2, :]
    marks = jnp.where(places == keys + 2 * CAP, list_ref[2:3, :].astype(f32), 0.0).astype(bf16)
    block = dot(marks, jnp.ones((list_pad, LANES), bf16))
    for half in range(width // LANES):
        hot = jnp.where(places == keys + half * CAP, 1.0, 0.0).astype(bf16)
        block = block + dot(hot, slot_total[:, half * LANES : (half + 1) * LANES])
    sh_out[...] = block.astype(bf16)
    own_grad = share_grad(rep)

    def slab(ref, peer):
        return ref.at[pl.ds(pl.multiple_of(peer * SLAB, SLAB), SLAB), :]

    def slab_copy(peer):
        return pltpu.make_async_remote_copy(
            src_ref=slab(sh_out, peer),
            dst_ref=slab(sh_in, me),
            send_sem=s_send.at[peer],
            recv_sem=s_recv.at[me],
            device_id=place(peer),
            device_id_type=MESH,
        )

    def slab_start(off, _):
        slab_copy(lax.rem(me + off, devices)).start()
        return 0

    lax.fori_loop(1, devices, slab_start, 0)
    own = pl.ds(pl.multiple_of(me * SLAB, SLAB), SLAB)
    sh_in[own, :] = sh_out[own, :]

    def slab_wait(off, _):
        peer = lax.rem(me + off, devices)
        pltpu.make_async_remote_copy(
            src_ref=slab(sh_out, peer),
            dst_ref=slab(sh_in, peer),
            send_sem=s_send.at[peer],
            recv_sem=s_recv.at[peer],
            device_id=place(peer),
            device_id_type=MESH,
        ).wait()
        return 0

    lax.fori_loop(1, devices, slab_wait, 0)
    inbound = sh_in[...]
    labels = jnp.transpose(inbound.astype(f32))[:SH_DEV, :]
    offset = lax.rem(lax.broadcasted_iota(jnp.int32, labels.shape, 1), SLAB)
    hot = labels == lax.broadcasted_iota(jnp.int32, labels.shape, 0).astype(f32)
    hot = jnp.where(hot & (offset >= 2 * CAP) & (offset < 3 * CAP), 1.0, 0.0)
    halves = []
    for half in range(width // LANES):
        moved = pltpu.roll(hot, hot.shape[1] - (2 - half) * CAP, 1)
        halves.append(dot(moved.astype(bf16), inbound))
    shared_grad = jnp.concatenate(halves, axis=1)
    state_cols = jnp.transpose(jnp.broadcast_to(sh_state_ref[...], (LANES, SH_DEV)))
    means = jnp.mean(shared_grad * shared_grad, axis=1, keepdims=True)
    new_state = state_cols + means
    new_sh_state_ref[...] = jnp.transpose(new_state)[0:1, :]
    own_shared = table_ref[pl.ds(pl.multiple_of(me * SH_DEV, SH_DEV), SH_DEV), :].astype(f32)
    new_sh_ref[...] = own_shared - learn_rate * shared_grad / jnp.sqrt(tiled(new_state, width))

    own = pl.ds(pl.multiple_of(rep * share, share), share)
    grad = own_grad
    for off in range(1, reps):
        peer = lax.rem(rep + reps - off, reps)
        pltpu.make_async_remote_copy(
            src_ref=rs_out.at[peer],
            dst_ref=rs_in.at[peer],
            send_sem=r_send.at[peer],
            recv_sem=r_recv.at[peer],
            device_id=(blk, peer),
            device_id_type=MESH,
        ).wait()
        grad = grad + rs_in[peer].astype(f32)
    new_state = ent_state_ref[...] + jnp.mean(grad * grad, axis=0, keepdims=True)
    new_ent_state_ref[...] = new_state
    update = jnp.transpose(learn_rate * grad / jnp.sqrt(new_state))
    new_ent_ref[...] = ent_ref[own, :].astype(f32) - update
    for bucket in range(1, buckets):
        id_copy(bucket).wait_send()
        query_copy(bucket).wait_send()
        grad_copy(bucket).wait_send()


def shards(
    entities,
    entity_state,
    shared_table,
    shared_state,
    edge_src,
    edge_dst,
    edge_slot,
    neg_rows,
    list_owner,
    list_row,
):
    reps = lax.axis_size("rep")
    devices = lax.axis_size("blk") * reps
    rows, width = entities.shape
    share = rows // reps
    buckets, edges = edge_src.shape[1:]
    groups = neg_rows.shape[2]
    list_pad = -(-list_row.shape[1] // LANES) * LANES
    sems = pltpu.SemaphoreType.DMA
    vmem = pl.BlockSpec(memory_space=pltpu.VMEM)
    new_entities, new_entity_state, new_shared, new_shared_state = pl.pallas_call(
        functools.partial(kernel, groups),
        out_shape=(
            jax.ShapeDtypeStruct((share, width), f32),
            jax.ShapeDtypeStruct((1, share), f32),
            jax.ShapeDtypeStruct((SH_DEV, width), f32),
            jax.ShapeDtypeStruct((1, SH_DEV), f32),
        ),
        in_specs=[vmem] * 10,
        out_specs=[vmem] * 4,
        scratch_shapes=[
            pltpu.VMEM((buckets, 8, edges), jnp.int32),
            pltpu.VMEM((8, list_pad), jnp.int32),
            pltpu.VMEM((width, rows), bf16),
            pltpu.VMEM((buckets * edges, rows), bf16),
            pltpu.VMEM((buckets, edges, list_pad), bf16),
            pltpu.VMEM((buckets, edges, width), bf16),
            pltpu.VMEM((buckets, edges, width), bf16),
            pltpu.VMEM((buckets, 8, edges), jnp.int32),
            pltpu.VMEM((buckets, width, edges), bf16),
            pltpu.VMEM((buckets, width, edges), bf16),
            pltpu.VMEM((edges, LANES), f32),
            pltpu.VMEM((groups * (rows // LANES), LANES), f32),
            pltpu.VMEM((edges, width), f32),
            pltpu.VMEM((width, rows), f32),
            pltpu.VMEM((reps, width, share), bf16),
            pltpu.VMEM((reps, width, share), bf16),
            pltpu.VMEM((devices * SLAB, LANES), bf16),
            pltpu.VMEM((devices * SLAB, LANES), bf16),
            sems((buckets,)),
            sems((buckets,)),
            sems((buckets,)),
            sems((buckets,)),
            sems((buckets,)),
            sems((buckets,)),
            sems((reps,)),
            sems((reps,)),
            sems((devices,)),
            sems((devices,)),
        ],
        compiler_params=pltpu.CompilerParams(
            collective_id=0, has_side_effects=True, vmem_limit_bytes=56 * 2**20
        ),
    )(
        entities,
        shared_table,
        edge_src,
        edge_dst,
        edge_slot,
        neg_rows,
        list_owner,
        list_row,
        entity_state.reshape(1, share),
        shared_state.reshape(1, SH_DEV),
    )
    return (
        new_entities,
        new_entity_state.reshape(share),
        new_shared,
        new_shared_state.reshape(SH_DEV),
    )


def solution(mesh):
    return jax.shard_map(
        shards,
        mesh=mesh,
        in_specs=(
            P("blk", None),
            P(("blk", "rep")),
            P(),
            P(("blk", "rep")),
            P("blk", None, "rep"),
            P("blk", None, "rep"),
            P("blk", None, "rep"),
            P("blk", None, "rep", None),
            P("blk", "rep", None),
            P("blk", "rep"),
        ),
        out_specs=(
            P(("blk", "rep"), None),
            P(("blk", "rep")),
            P(("blk", "rep"), None),
            P(("blk", "rep")),
        ),
        check_vma=False,
    )
```

```python
import functools

import jax
import jax.numpy as jnp
from jax import lax
from jax.experimental import pallas as pl
from jax.experimental.pallas import tpu as pltpu
from jax.sharding import PartitionSpec as P

CAP = 4
SH_DEV = 64
LANES = 128
HALVES = 2
CHUNK = 512
SLAB = 16


learn_rate = 0.1
negative_weight = 8.0
MESH = pl.DeviceIdType.MESH
f32 = jnp.float32
bf16 = jnp.bfloat16


def dot(a, b):
    return jnp.dot(a, b, preferred_element_type=f32)


def columns(row):
    return jnp.transpose(jnp.broadcast_to(row.astype(f32), (LANES, row.shape[1])))


def tiled(cols, width):
    return jnp.concatenate([cols] * (width // LANES), axis=1)


def lane_hot(cols, start, width):
    ids = lax.broadcasted_iota(jnp.int32, (cols.shape[0], width), 1) + start
    return tiled(cols, width) == ids.astype(f32)


def kernel(
    groups,
    ent_ref,
    table_ref,
    src_ref,
    dst_ref,
    slots_ref,
    neg_ref,
    owner_ref,
    row_ref,
    ent_state_ref,
    sh_state_ref,
    new_ent_ref,
    new_ent_state_ref,
    new_sh_ref,
    new_sh_state_ref,
    ids_ref,
    list_ref,
    vt_ref,
    pick_ref,
    slot_ref,
    q_out,
    q_in,
    ids_in,
    qg_out,
    qg_in,
    dcol_ref,
    cnt_ref,
    qg_ref,
    gt_ref,
    rs_out,
    rs_in,
    sh_out,
    sh_in,
    q_send,
    q_recv,
    i_send,
    i_recv,
    g_send,
    g_recv,
    r_send,
    r_recv,
    s_send,
    s_recv,
):
    blk, rep = lax.axis_index("blk"), lax.axis_index("rep")
    blks, reps = lax.axis_size("blk"), lax.axis_size("rep")
    devices = blks * reps
    me = blk * reps + rep
    rows, width = ent_ref.shape
    buckets, edges = src_ref.shape[1:]
    group_edges = edges // groups
    chunks = rows // CHUNK
    highs = rows // LANES
    share = rows // reps
    part = width // HALVES
    list_pad = list_ref.shape[1]

    def place(peer):
        return (peer // reps, lax.rem(peer, reps))

    barrier = pltpu.get_barrier_semaphore()

    def greet(off, _):
        pl.semaphore_signal(
            barrier,
            inc=1,
            device_id=place(lax.rem(me + off, devices)),
            device_id_type=MESH,
        )
        return 0

    lax.fori_loop(1, devices, greet, 0)

    for bucket in range(buckets):
        ids_ref[bucket, 0:1, :] = dst_ref[0, bucket : bucket + 1, :]
        ids_ref[bucket, 1 : 1 + groups, :] = neg_ref[0, bucket]
        ids_ref[bucket, 1 + groups : 2 + groups, :] = src_ref[0, bucket : bucket + 1, :]
        ids_ref[bucket, 2 + groups : 3 + groups, :] = slots_ref[0, bucket : bucket + 1, :]
        ids_ref[bucket, 3 + groups :, :] = jnp.zeros((8 - 3 - groups, edges), jnp.int32)
    count = row_ref.shape[1]
    owners = owner_ref[...]
    owner_cols = jnp.concatenate([columns(owners)] * (list_ref.shape[1] // LANES), axis=1)
    same = owner_cols[:, :count] == owners.astype(f32)
    earlier = lax.broadcasted_iota(jnp.int32, (count, count), 0) < lax.broadcasted_iota(
        jnp.int32, (count, count), 1
    )
    ranks = jnp.sum(jnp.where(same & earlier, 1.0, 0.0), axis=0, keepdims=True)
    list_ref[...] = jnp.full(list_ref.shape, -SH_DEV, jnp.int32)
    list_ref[0:1, :count] = owners * SH_DEV + row_ref[...]
    list_ref[1:2, :count] = owners * SLAB + ranks.astype(jnp.int32)
    list_ref[2:3, :count] = row_ref[...]

    vt_ref[...] = jnp.transpose(ent_ref[...].astype(f32)).astype(bf16)
    id_cols = columns(list_ref[0:1, :])
    shared_rows = jnp.zeros((list_pad, width), f32)
    step = min(2048, table_ref.shape[0])
    for start in range(0, table_ref.shape[0], step):
        hot = jnp.where(lane_hot(id_cols, start, step), 1.0, 0.0).astype(bf16)
        shared_rows = shared_rows + dot(hot, table_ref[start : start + step, :])
    shared_rows = shared_rows.astype(bf16)

    def to_back(bucket):
        return (lax.rem(blk - bucket + blks, blks), rep)

    def to_front(bucket):
        return (lax.rem(blk + bucket, blks), rep)

    def id_copy(bucket):
        return pltpu.make_async_remote_copy(
            src_ref=ids_ref.at[bucket],
            dst_ref=ids_in.at[bucket],
            send_sem=i_send.at[bucket],
            recv_sem=i_recv.at[bucket],
            device_id=to_back(bucket),
            device_id_type=MESH,
        )

    def query_copy(bucket):
        return pltpu.make_async_remote_copy(
            src_ref=q_out.at[bucket],
            dst_ref=q_in.at[bucket],
            send_sem=q_send.at[bucket],
            recv_sem=q_recv.at[bucket],
            device_id=to_back(bucket),
            device_id_type=MESH,
        )

    def grad_copy(bucket, half):
        place = half * buckets + bucket
        return pltpu.make_async_remote_copy(
            src_ref=qg_out.at[place],
            dst_ref=qg_in.at[place],
            send_sem=g_send.at[place],
            recv_sem=g_recv.at[place],
            device_id=to_front(bucket),
            device_id_type=MESH,
        )

    def make_query(bucket):
        slot = jnp.where(lane_hot(columns(ids_ref[bucket, 2 + groups : 3 + groups, :]), 0, list_pad), 1.0, 0.0)
        slot_ref[bucket] = slot.astype(bf16)
        dcol_ref[...] = columns(ids_ref[bucket, 1 + groups : 2 + groups, :])
        qg_ref[...] = dot(slot_ref[bucket], shared_rows)

        def body(c, _):
            at = pl.multiple_of(c * CHUNK, CHUNK)
            pick = jnp.where(lane_hot(dcol_ref[...], at, CHUNK), 1.0, 0.0).astype(bf16)
            pick_ref[bucket * edges : (bucket + 1) * edges, pl.ds(at, CHUNK)] = pick
            qg_ref[...] += dot(pick, ent_ref[pl.ds(at, CHUNK), :])
            return 0

        lax.fori_loop(0, chunks, body, 0, unroll=True)
        q_out[bucket] = qg_ref[...].astype(bf16)

    def score(query_ref, id_ref, bucket):
        query = query_ref[...]
        query_t = jnp.transpose(query.astype(f32)).astype(bf16)
        dcol_ref[...] = columns(id_ref[0:1, :])
        for g in range(groups):
            ids = id_ref[1 + g : 2 + g, :]
            high = lax.broadcasted_iota(jnp.int32, (highs, ids.shape[1]), 0) == ids // LANES
            low = lax.broadcasted_iota(jnp.int32, (LANES, ids.shape[1]), 0) == lax.rem(ids, LANES)
            counts = lax.dot_general(
                jnp.where(high, 1.0, 0.0).astype(bf16),
                jnp.where(low, 1.0, 0.0).astype(bf16),
                (((1,), (1,)), ((), ())),
                preferred_element_type=f32,
            )
            cnt_ref[g * highs : (g + 1) * highs, :] = counts * (negative_weight / ids.shape[1])
        qg_ref[...] = jnp.zeros_like(qg_ref)

        def body(c, _):
            at = pl.multiple_of(c * CHUNK, CHUNK)
            scores = dot(query, vt_ref[:, pl.ds(at, CHUNK)])
            sigmoid = 0.5 * jnp.tanh(0.5 * scores) + 0.5
            per = CHUNK // LANES
            counts = jnp.concatenate(
                [
                    jnp.concatenate(
                        [
                            jnp.broadcast_to(
                                cnt_ref[pl.ds(g * highs + c * per + h, 1), :],
                                (group_edges, LANES),
                            )
                            for h in range(per)
                        ],
                        axis=1,
                    )
                    for g in range(groups)
                ],
                axis=0,
            )
            target = lane_hot(dcol_ref[...], at, CHUNK)
            sampled = sigmoid * counts
            weight = jnp.where(target, sampled + sigmoid - 1.0, sampled).astype(bf16)
            qg_ref[...] += dot(weight, ent_ref[pl.ds(at, CHUNK), :])
            grown = dot(query_t, weight)
            if bucket == 0:
                gt_ref[:, pl.ds(at, CHUNK)] = grown
            else:
                gt_ref[:, pl.ds(at, CHUNK)] += grown
            return 0

        lax.fori_loop(0, chunks, body, 0, unroll=True)
        grads = jnp.transpose(qg_ref[...]).astype(bf16)
        for half in range(HALVES):
            qg_out[half * buckets + bucket] = grads[half * part : (half + 1) * part, :]

    make_query(1)
    pl.semaphore_wait(barrier, devices - 1)
    for bucket in range(1, buckets):
        id_copy(bucket).start()
    for bucket in range(1, buckets):
        if bucket > 1:
            make_query(bucket)
        query_copy(bucket).start()
    make_query(0)
    score(q_out.at[0], ids_ref.at[0], 0)
    for bucket in range(1, buckets):
        id_copy(bucket).wait_recv()
        query_copy(bucket).wait_recv()
        score(q_in.at[bucket], ids_in.at[bucket], bucket)
        grad_copy(bucket, 0).start()
    for half in range(1, HALVES):
        for bucket in range(1, buckets):
            grad_copy(bucket, half).start()

    def share_copy(peer, half, slot):
        return pltpu.make_async_remote_copy(
            src_ref=rs_out.at[half * reps + peer],
            dst_ref=rs_in.at[half * reps + slot],
            send_sem=r_send.at[half * reps + peer],
            recv_sem=r_recv.at[half * reps + slot],
            device_id=(blk, peer),
            device_id_type=MESH,
        )

    backs, own_grad = [], []
    for half in range(HALVES):
        for bucket in range(1, buckets):
            grad_copy(bucket, half).wait_recv()
        back = [qg_out[half * buckets]]
        back = back + [qg_in[half * buckets + bucket] for bucket in range(1, buckets)]
        back = jnp.concatenate(back, axis=1)
        backs.append(back)

        def share_grad(peer, half=half, back=back):
            at = pl.ds(pl.multiple_of(peer * share, share), share)
            return gt_ref[half * part : (half + 1) * part, at] + dot(back, pick_ref[:, at])

        for off in range(1, reps):
            peer = lax.rem(rep + off, reps)
            rs_out[half * reps + peer] = share_grad(peer).astype(bf16)
            share_copy(peer, half, rep).start()
        own_grad.append(share_grad(rep))
    own_grad = jnp.concatenate(own_grad, axis=0)
    backs = jnp.concatenate(backs, axis=0)

    slot_total = jnp.zeros((width, list_pad), f32)
    for bucket in range(buckets):
        back = backs[:, bucket * edges : (bucket + 1) * edges]
        slot_total = slot_total + dot(back, slot_ref[bucket])
    slot_total = jnp.transpose(slot_total).astype(bf16)
    places = lax.broadcasted_iota(jnp.int32, (devices * SLAB, list_pad), 0)
    keys = list_ref[1:2, :]
    marks = jnp.where(places == keys + 2 * CAP, list_ref[2:3, :].astype(f32), 0.0).astype(bf16)
    block = dot(marks, jnp.ones((list_pad, LANES), bf16))
    for half in range(width // LANES):
        hot = jnp.where(places == keys + half * CAP, 1.0, 0.0).astype(bf16)
        block = block + dot(hot, slot_total[:, half * LANES : (half + 1) * LANES])
    sh_out[...] = block.astype(bf16)

    def slab(ref, peer):
        return ref.at[pl.ds(pl.multiple_of(peer * SLAB, SLAB), SLAB), :]

    def slab_copy(peer):
        return pltpu.make_async_remote_copy(
            src_ref=slab(sh_out, peer),
            dst_ref=slab(sh_in, me),
            send_sem=s_send.at[peer],
            recv_sem=s_recv.at[me],
            device_id=place(peer),
            device_id_type=MESH,
        )

    def slab_start(off, _):
        slab_copy(lax.rem(me + off, devices)).start()
        return 0

    lax.fori_loop(1, devices, slab_start, 0)
    own = pl.ds(pl.multiple_of(me * SLAB, SLAB), SLAB)
    sh_in[own, :] = sh_out[own, :]

    def slab_wait(off, _):
        peer = lax.rem(me + off, devices)
        pltpu.make_async_remote_copy(
            src_ref=slab(sh_out, peer),
            dst_ref=slab(sh_in, peer),
            send_sem=s_send.at[peer],
            recv_sem=s_recv.at[peer],
            device_id=place(peer),
            device_id_type=MESH,
        ).wait()
        return 0

    lax.fori_loop(1, devices, slab_wait, 0)
    inbound = sh_in[...]
    labels = jnp.transpose(inbound.astype(f32))[:SH_DEV, :]
    offset = lax.rem(lax.broadcasted_iota(jnp.int32, labels.shape, 1), SLAB)
    hot = labels == lax.broadcasted_iota(jnp.int32, labels.shape, 0).astype(f32)
    hot = jnp.where(hot & (offset >= 2 * CAP) & (offset < 3 * CAP), 1.0, 0.0)
    halves = []
    for half in range(width // LANES):
        moved = pltpu.roll(hot, hot.shape[1] - (2 - half) * CAP, 1)
        halves.append(dot(moved.astype(bf16), inbound))
    shared_grad = jnp.concatenate(halves, axis=1)
    state_cols = jnp.transpose(jnp.broadcast_to(sh_state_ref[...], (LANES, SH_DEV)))
    means = jnp.mean(shared_grad * shared_grad, axis=1, keepdims=True)
    new_state = state_cols + means
    new_sh_state_ref[...] = jnp.transpose(new_state)[0:1, :]
    own_shared = table_ref[pl.ds(pl.multiple_of(me * SH_DEV, SH_DEV), SH_DEV), :].astype(f32)
    new_sh_ref[...] = own_shared - learn_rate * shared_grad / jnp.sqrt(tiled(new_state, width))

    own = pl.ds(pl.multiple_of(rep * share, share), share)
    grad = own_grad
    for off in range(1, reps):
        peer = lax.rem(rep + reps - off, reps)
        arrived = []
        for half in range(HALVES):
            share_copy(peer, half, peer).wait()
            arrived.append(rs_in[half * reps + peer].astype(f32))
        grad = grad + jnp.concatenate(arrived, axis=0)
    new_state = ent_state_ref[...] + jnp.mean(grad * grad, axis=0, keepdims=True)
    new_ent_state_ref[...] = new_state
    update = jnp.transpose(learn_rate * grad / jnp.sqrt(new_state))
    new_ent_ref[...] = ent_ref[own, :].astype(f32) - update
    for bucket in range(1, buckets):
        id_copy(bucket).wait_send()
        query_copy(bucket).wait_send()
        for half in range(HALVES):
            grad_copy(bucket, half).wait_send()


def shards(
    entities,
    entity_state,
    shared_table,
    shared_state,
    edge_src,
    edge_dst,
    edge_slot,
    neg_rows,
    list_owner,
    list_row,
):
    reps = lax.axis_size("rep")
    devices = lax.axis_size("blk") * reps
    rows, width = entities.shape
    share = rows // reps
    buckets, edges = edge_src.shape[1:]
    groups = neg_rows.shape[2]
    list_pad = -(-list_row.shape[1] // LANES) * LANES
    sems = pltpu.SemaphoreType.DMA
    vmem = pl.BlockSpec(memory_space=pltpu.VMEM)
    new_entities, new_entity_state, new_shared, new_shared_state = pl.pallas_call(
        functools.partial(kernel, groups),
        out_shape=(
            jax.ShapeDtypeStruct((share, width), f32),
            jax.ShapeDtypeStruct((1, share), f32),
            jax.ShapeDtypeStruct((SH_DEV, width), f32),
            jax.ShapeDtypeStruct((1, SH_DEV), f32),
        ),
        in_specs=[vmem] * 10,
        out_specs=[vmem] * 4,
        scratch_shapes=[
            pltpu.VMEM((buckets, 8, edges), jnp.int32),
            pltpu.VMEM((8, list_pad), jnp.int32),
            pltpu.VMEM((width, rows), bf16),
            pltpu.VMEM((buckets * edges, rows), bf16),
            pltpu.VMEM((buckets, edges, list_pad), bf16),
            pltpu.VMEM((buckets, edges, width), bf16),
            pltpu.VMEM((buckets, edges, width), bf16),
            pltpu.VMEM((buckets, 8, edges), jnp.int32),
            pltpu.VMEM((HALVES * buckets, width // HALVES, edges), bf16),
            pltpu.VMEM((HALVES * buckets, width // HALVES, edges), bf16),
            pltpu.VMEM((edges, LANES), f32),
            pltpu.VMEM((groups * (rows // LANES), LANES), f32),
            pltpu.VMEM((edges, width), f32),
            pltpu.VMEM((width, rows), f32),
            pltpu.VMEM((HALVES * reps, width // HALVES, share), bf16),
            pltpu.VMEM((HALVES * reps, width // HALVES, share), bf16),
            pltpu.VMEM((devices * SLAB, LANES), bf16),
            pltpu.VMEM((devices * SLAB, LANES), bf16),
            sems((buckets,)),
            sems((buckets,)),
            sems((buckets,)),
            sems((buckets,)),
            sems((HALVES * buckets,)),
            sems((HALVES * buckets,)),
            sems((HALVES * reps,)),
            sems((HALVES * reps,)),
            sems((devices,)),
            sems((devices,)),
        ],
        compiler_params=pltpu.CompilerParams(
            collective_id=0, has_side_effects=True, vmem_limit_bytes=56 * 2**20
        ),
    )(
        entities,
        shared_table,
        edge_src,
        edge_dst,
        edge_slot,
        neg_rows,
        list_owner.reshape(list_row.shape),
        list_row,
        entity_state.reshape(1, share),
        shared_state.reshape(1, SH_DEV),
    )
    return (
        new_entities,
        new_entity_state.reshape(share),
        new_shared,
        new_shared_state.reshape(SH_DEV),
    )


def solution(mesh):
    return jax.shard_map(
        shards,
        mesh=mesh,
        in_specs=(
            P("blk", None),
            P(("blk", "rep")),
            P(),
            P(("blk", "rep")),
            P("blk", None, "rep"),
            P("blk", None, "rep"),
            P("blk", None, "rep"),
            P("blk", None, "rep", None),
            P("blk", "rep", None),
            P("blk", "rep"),
        ),
        out_specs=(
            P(("blk", "rep"), None),
            P(("blk", "rep")),
            P(("blk", "rep"), None),
            P(("blk", "rep")),
        ),
        check_vma=False,
    )
```

```python
import functools

import jax
import jax.numpy as jnp
from jax import lax
from jax.experimental import pallas as pl
from jax.experimental.pallas import tpu as pltpu
from jax.sharding import PartitionSpec as P

CAP = 4
SH_DEV = 64
LANES = 128
HALVES = 2
CHUNK = 512
SLAB = 16


learn_rate = 0.1
negative_weight = 8.0
MESH = pl.DeviceIdType.MESH
f32 = jnp.float32
bf16 = jnp.bfloat16


def dot(a, b):
    return jnp.dot(a, b, preferred_element_type=f32)


def columns(row):
    return jnp.transpose(jnp.broadcast_to(row.astype(f32), (LANES, row.shape[1])))


def tiled(cols, width):
    return jnp.concatenate([cols] * (width // LANES), axis=1)


def lane_hot(cols, start, width):
    ids = lax.broadcasted_iota(jnp.int32, (cols.shape[0], width), 1) + start
    return tiled(cols, width) == ids.astype(f32)


def kernel(
    groups,
    ent_ref,
    table_ref,
    src_ref,
    dst_ref,
    slots_ref,
    neg_ref,
    owner_ref,
    row_ref,
    ent_state_ref,
    sh_state_ref,
    new_ent_ref,
    new_ent_state_ref,
    new_sh_ref,
    new_sh_state_ref,
    ids_ref,
    list_ref,
    vt_ref,
    pick_ref,
    slot_ref,
    q_out,
    q_in,
    ids_in,
    qg_out,
    qg_in,
    dcol_ref,
    cnt_ref,
    qg_ref,
    gt_ref,
    rs_out,
    rs_up,
    rs_down,
    own_ref,
    sh_out,
    sh_in,
    q_send,
    q_recv,
    i_send,
    i_recv,
    g_send,
    g_recv,
    r_send,
    up_recv,
    down_recv,
    s_send,
    s_recv,
):
    blk, rep = lax.axis_index("blk"), lax.axis_index("rep")
    blks, reps = lax.axis_size("blk"), lax.axis_size("rep")
    devices = blks * reps
    me = blk * reps + rep
    rows, width = ent_ref.shape
    buckets, edges = src_ref.shape[1:]
    group_edges = edges // groups
    chunks = rows // CHUNK
    highs = rows // LANES
    share = rows // reps
    part = width // HALVES
    list_pad = list_ref.shape[1]

    def place(peer):
        return (peer // reps, lax.rem(peer, reps))

    barrier = pltpu.get_barrier_semaphore()

    def greet(off, _):
        pl.semaphore_signal(
            barrier,
            inc=1,
            device_id=place(lax.rem(me + off, devices)),
            device_id_type=MESH,
        )
        return 0

    lax.fori_loop(1, devices, greet, 0)

    for bucket in range(buckets):
        ids_ref[bucket, 0:1, :] = dst_ref[0, bucket : bucket + 1, :]
        ids_ref[bucket, 1 : 1 + groups, :] = neg_ref[0, bucket]
        ids_ref[bucket, 1 + groups : 2 + groups, :] = src_ref[0, bucket : bucket + 1, :]
        ids_ref[bucket, 2 + groups : 3 + groups, :] = slots_ref[0, bucket : bucket + 1, :]
        ids_ref[bucket, 3 + groups :, :] = jnp.zeros((8 - 3 - groups, edges), jnp.int32)
    count = row_ref.shape[1]
    owners = owner_ref[...]
    owner_cols = jnp.concatenate([columns(owners)] * (list_ref.shape[1] // LANES), axis=1)
    same = owner_cols[:, :count] == owners.astype(f32)
    earlier = lax.broadcasted_iota(jnp.int32, (count, count), 0) < lax.broadcasted_iota(
        jnp.int32, (count, count), 1
    )
    ranks = jnp.sum(jnp.where(same & earlier, 1.0, 0.0), axis=0, keepdims=True)
    list_ref[...] = jnp.full(list_ref.shape, -SH_DEV, jnp.int32)
    list_ref[0:1, :count] = owners * SH_DEV + row_ref[...]
    list_ref[1:2, :count] = owners * SLAB + ranks.astype(jnp.int32)
    list_ref[2:3, :count] = row_ref[...]

    vt_ref[...] = jnp.transpose(ent_ref[...].astype(f32)).astype(bf16)
    id_cols = columns(list_ref[0:1, :])
    shared_rows = jnp.zeros((list_pad, width), f32)
    step = min(2048, table_ref.shape[0])
    for start in range(0, table_ref.shape[0], step):
        hot = jnp.where(lane_hot(id_cols, start, step), 1.0, 0.0).astype(bf16)
        shared_rows = shared_rows + dot(hot, table_ref[start : start + step, :])
    shared_rows = shared_rows.astype(bf16)

    def to_back(bucket):
        return (lax.rem(blk - bucket + blks, blks), rep)

    def to_front(bucket):
        return (lax.rem(blk + bucket, blks), rep)

    def id_copy(bucket):
        return pltpu.make_async_remote_copy(
            src_ref=ids_ref.at[bucket],
            dst_ref=ids_in.at[bucket],
            send_sem=i_send.at[bucket],
            recv_sem=i_recv.at[bucket],
            device_id=to_back(bucket),
            device_id_type=MESH,
        )

    def query_copy(bucket):
        return pltpu.make_async_remote_copy(
            src_ref=q_out.at[bucket],
            dst_ref=q_in.at[bucket],
            send_sem=q_send.at[bucket],
            recv_sem=q_recv.at[bucket],
            device_id=to_back(bucket),
            device_id_type=MESH,
        )

    def grad_copy(bucket, half):
        place = half * buckets + bucket
        return pltpu.make_async_remote_copy(
            src_ref=qg_out.at[place],
            dst_ref=qg_in.at[place],
            send_sem=g_send.at[place],
            recv_sem=g_recv.at[place],
            device_id=to_front(bucket),
            device_id_type=MESH,
        )

    def make_query(bucket):
        slot = jnp.where(lane_hot(columns(ids_ref[bucket, 2 + groups : 3 + groups, :]), 0, list_pad), 1.0, 0.0)
        slot_ref[bucket] = slot.astype(bf16)
        dcol_ref[...] = columns(ids_ref[bucket, 1 + groups : 2 + groups, :])
        qg_ref[...] = dot(slot_ref[bucket], shared_rows)

        def body(c, _):
            at = pl.multiple_of(c * CHUNK, CHUNK)
            pick = jnp.where(lane_hot(dcol_ref[...], at, CHUNK), 1.0, 0.0).astype(bf16)
            pick_ref[bucket * edges : (bucket + 1) * edges, pl.ds(at, CHUNK)] = pick
            qg_ref[...] += dot(pick, ent_ref[pl.ds(at, CHUNK), :])
            return 0

        lax.fori_loop(0, chunks, body, 0, unroll=True)
        q_out[bucket] = qg_ref[...].astype(bf16)

    def score(query_ref, id_ref, bucket):
        query = query_ref[...]
        query_t = jnp.transpose(query.astype(f32)).astype(bf16)
        dcol_ref[...] = columns(id_ref[0:1, :])
        for g in range(groups):
            ids = id_ref[1 + g : 2 + g, :]
            high = lax.broadcasted_iota(jnp.int32, (highs, ids.shape[1]), 0) == ids // LANES
            low = lax.broadcasted_iota(jnp.int32, (LANES, ids.shape[1]), 0) == lax.rem(ids, LANES)
            counts = lax.dot_general(
                jnp.where(high, 1.0, 0.0).astype(bf16),
                jnp.where(low, 1.0, 0.0).astype(bf16),
                (((1,), (1,)), ((), ())),
                preferred_element_type=f32,
            )
            cnt_ref[g * highs : (g + 1) * highs, :] = counts * (negative_weight / ids.shape[1])
        qg_ref[...] = jnp.zeros_like(qg_ref)

        def body(c, _):
            at = pl.multiple_of(c * CHUNK, CHUNK)
            scores = dot(query, vt_ref[:, pl.ds(at, CHUNK)])
            sigmoid = 0.5 * jnp.tanh(0.5 * scores) + 0.5
            per = CHUNK // LANES
            counts = jnp.concatenate(
                [
                    jnp.concatenate(
                        [
                            jnp.broadcast_to(
                                cnt_ref[pl.ds(g * highs + c * per + h, 1), :],
                                (group_edges, LANES),
                            )
                            for h in range(per)
                        ],
                        axis=1,
                    )
                    for g in range(groups)
                ],
                axis=0,
            )
            target = lane_hot(dcol_ref[...], at, CHUNK)
            sampled = sigmoid * counts
            weight = jnp.where(target, sampled + sigmoid - 1.0, sampled).astype(bf16)
            qg_ref[...] += dot(weight, ent_ref[pl.ds(at, CHUNK), :])
            grown = dot(query_t, weight)
            if bucket == 0:
                gt_ref[:, pl.ds(at, CHUNK)] = grown
            else:
                gt_ref[:, pl.ds(at, CHUNK)] += grown
            return 0

        lax.fori_loop(0, chunks, body, 0, unroll=True)
        grads = jnp.transpose(qg_ref[...]).astype(bf16)
        for half in range(HALVES):
            qg_out[half * buckets + bucket] = grads[half * part : (half + 1) * part, :]

    make_query(1)
    pl.semaphore_wait(barrier, devices - 1)
    for bucket in range(1, buckets):
        id_copy(bucket).start()
    for bucket in range(1, buckets):
        if bucket > 1:
            make_query(bucket)
        query_copy(bucket).start()
    make_query(0)
    score(q_out.at[0], ids_ref.at[0], 0)
    for bucket in range(1, buckets):
        id_copy(bucket).wait_recv()
        query_copy(bucket).wait_recv()
        score(q_in.at[bucket], ids_in.at[bucket], bucket)
        grad_copy(bucket, 0).start()
    for half in range(1, HALVES):
        for bucket in range(1, buckets):
            grad_copy(bucket, half).start()

    def share_copy(half, peer, up):
        at = half * reps + peer
        return pltpu.make_async_remote_copy(
            src_ref=rs_out.at[at],
            dst_ref=(rs_up if up else rs_down).at[at],
            send_sem=r_send.at[at],
            recv_sem=(up_recv if up else down_recv).at[at],
            device_id=(blk, lax.rem(rep + (1 if up else reps - 1), reps)),
            device_id_type=MESH,
        )

    def pass_share(half, peer, up, taken, share_grad):
        at = half * reps + peer
        first = rep == (0 if up else reps - 1)

        @pl.when(taken & (rep < peer if up else rep > peer))
        def _():
            total = share_grad(peer)

            @pl.when(first)
            def _():
                rs_out[at] = total.astype(bf16)

            @pl.when(jnp.logical_not(first))
            def _():
                share_copy(half, peer, up).wait_recv()
                rs_out[at] = (total + (rs_up if up else rs_down)[at].astype(f32)).astype(bf16)

            share_copy(half, peer, up).start()

    backs = []
    low_end = rep < reps // 2
    for half in range(HALVES):
        for bucket in range(1, buckets):
            grad_copy(bucket, half).wait_recv()
        back = [qg_out[half * buckets]]
        back = back + [qg_in[half * buckets + bucket] for bucket in range(1, buckets)]
        back = jnp.concatenate(back, axis=1)
        backs.append(back)

        def share_grad(peer, half=half, back=back):
            at = pl.ds(pl.multiple_of(peer * share, share), share)
            return gt_ref[half * part : (half + 1) * part, at] + dot(back, pick_ref[:, at])

        for hop in range(reps - 1):
            pass_share(half, reps - 1 - hop, True, low_end, share_grad)
            pass_share(half, hop, False, rep >= 0, share_grad)
            pass_share(half, reps - 1 - hop, True, jnp.logical_not(low_end), share_grad)
        own_ref[half * part : (half + 1) * part, :] = share_grad(rep)
    backs = jnp.concatenate(backs, axis=0)

    slot_total = jnp.zeros((width, list_pad), f32)
    for bucket in range(buckets):
        back = backs[:, bucket * edges : (bucket + 1) * edges]
        slot_total = slot_total + dot(back, slot_ref[bucket])
    slot_total = jnp.transpose(slot_total).astype(bf16)
    places = lax.broadcasted_iota(jnp.int32, (devices * SLAB, list_pad), 0)
    keys = list_ref[1:2, :]
    marks = jnp.where(places == keys + 2 * CAP, list_ref[2:3, :].astype(f32), 0.0).astype(bf16)
    block = dot(marks, jnp.ones((list_pad, LANES), bf16))
    for half in range(width // LANES):
        hot = jnp.where(places == keys + half * CAP, 1.0, 0.0).astype(bf16)
        block = block + dot(hot, slot_total[:, half * LANES : (half + 1) * LANES])
    sh_out[...] = block.astype(bf16)

    def slab(ref, peer):
        return ref.at[pl.ds(pl.multiple_of(peer * SLAB, SLAB), SLAB), :]

    def slab_copy(peer):
        return pltpu.make_async_remote_copy(
            src_ref=slab(sh_out, peer),
            dst_ref=slab(sh_in, me),
            send_sem=s_send.at[peer],
            recv_sem=s_recv.at[me],
            device_id=place(peer),
            device_id_type=MESH,
        )

    def slab_start(off, _):
        slab_copy(lax.rem(me + off, devices)).start()
        return 0

    lax.fori_loop(1, devices, slab_start, 0)
    own = pl.ds(pl.multiple_of(me * SLAB, SLAB), SLAB)
    sh_in[own, :] = sh_out[own, :]

    def slab_wait(off, _):
        peer = lax.rem(me + off, devices)
        pltpu.make_async_remote_copy(
            src_ref=slab(sh_out, peer),
            dst_ref=slab(sh_in, peer),
            send_sem=s_send.at[peer],
            recv_sem=s_recv.at[peer],
            device_id=place(peer),
            device_id_type=MESH,
        ).wait()
        return 0

    lax.fori_loop(1, devices, slab_wait, 0)
    inbound = sh_in[...]
    labels = jnp.transpose(inbound.astype(f32))[:SH_DEV, :]
    offset = lax.rem(lax.broadcasted_iota(jnp.int32, labels.shape, 1), SLAB)
    hot = labels == lax.broadcasted_iota(jnp.int32, labels.shape, 0).astype(f32)
    hot = jnp.where(hot & (offset >= 2 * CAP) & (offset < 3 * CAP), 1.0, 0.0)
    halves = []
    for half in range(width // LANES):
        moved = pltpu.roll(hot, hot.shape[1] - (2 - half) * CAP, 1)
        halves.append(dot(moved.astype(bf16), inbound))
    shared_grad = jnp.concatenate(halves, axis=1)
    state_cols = jnp.transpose(jnp.broadcast_to(sh_state_ref[...], (LANES, SH_DEV)))
    means = jnp.mean(shared_grad * shared_grad, axis=1, keepdims=True)
    new_state = state_cols + means
    new_sh_state_ref[...] = jnp.transpose(new_state)[0:1, :]
    own_shared = table_ref[pl.ds(pl.multiple_of(me * SH_DEV, SH_DEV), SH_DEV), :].astype(f32)
    new_sh_ref[...] = own_shared - learn_rate * shared_grad / jnp.sqrt(tiled(new_state, width))

    own = pl.ds(pl.multiple_of(rep * share, share), share)
    for up in (True, False):

        @pl.when((rep > 0) if up else (rep < reps - 1))
        def _(up=up):
            for half in range(HALVES):
                share_copy(half, rep, up).wait_recv()
                arrived = (rs_up if up else rs_down)[half * reps + rep]
                own_ref[half * part : (half + 1) * part, :] += arrived.astype(f32)

    grad = own_ref[...]
    new_state = ent_state_ref[...] + jnp.mean(grad * grad, axis=0, keepdims=True)
    new_ent_state_ref[...] = new_state
    update = jnp.transpose(learn_rate * grad / jnp.sqrt(new_state))
    new_ent_ref[...] = ent_ref[own, :].astype(f32) - update
    for bucket in range(1, buckets):
        id_copy(bucket).wait_send()
        query_copy(bucket).wait_send()
        for half in range(HALVES):
            grad_copy(bucket, half).wait_send()
    for peer in range(reps):

        @pl.when(rep != peer)
        def _(peer=peer):
            for half in range(HALVES):
                share_copy(half, peer, True).wait_send()


def shards(
    entities,
    entity_state,
    shared_table,
    shared_state,
    edge_src,
    edge_dst,
    edge_slot,
    neg_rows,
    list_owner,
    list_row,
):
    reps = lax.axis_size("rep")
    devices = lax.axis_size("blk") * reps
    rows, width = entities.shape
    share = rows // reps
    buckets, edges = edge_src.shape[1:]
    groups = neg_rows.shape[2]
    list_pad = -(-list_row.shape[1] // LANES) * LANES
    sems = pltpu.SemaphoreType.DMA
    vmem = pl.BlockSpec(memory_space=pltpu.VMEM)
    new_entities, new_entity_state, new_shared, new_shared_state = pl.pallas_call(
        functools.partial(kernel, groups),
        out_shape=(
            jax.ShapeDtypeStruct((share, width), f32),
            jax.ShapeDtypeStruct((1, share), f32),
            jax.ShapeDtypeStruct((SH_DEV, width), f32),
            jax.ShapeDtypeStruct((1, SH_DEV), f32),
        ),
        in_specs=[vmem] * 10,
        out_specs=[vmem] * 4,
        scratch_shapes=[
            pltpu.VMEM((buckets, 8, edges), jnp.int32),
            pltpu.VMEM((8, list_pad), jnp.int32),
            pltpu.VMEM((width, rows), bf16),
            pltpu.VMEM((buckets * edges, rows), bf16),
            pltpu.VMEM((buckets, edges, list_pad), bf16),
            pltpu.VMEM((buckets, edges, width), bf16),
            pltpu.VMEM((buckets, edges, width), bf16),
            pltpu.VMEM((buckets, 8, edges), jnp.int32),
            pltpu.VMEM((HALVES * buckets, width // HALVES, edges), bf16),
            pltpu.VMEM((HALVES * buckets, width // HALVES, edges), bf16),
            pltpu.VMEM((edges, LANES), f32),
            pltpu.VMEM((groups * (rows // LANES), LANES), f32),
            pltpu.VMEM((edges, width), f32),
            pltpu.VMEM((width, rows), f32),
            pltpu.VMEM((HALVES * reps, width // HALVES, share), bf16),
            pltpu.VMEM((HALVES * reps, width // HALVES, share), bf16),
            pltpu.VMEM((HALVES * reps, width // HALVES, share), bf16),
            pltpu.VMEM((width, share), f32),
            pltpu.VMEM((devices * SLAB, LANES), bf16),
            pltpu.VMEM((devices * SLAB, LANES), bf16),
            sems((buckets,)),
            sems((buckets,)),
            sems((buckets,)),
            sems((buckets,)),
            sems((HALVES * buckets,)),
            sems((HALVES * buckets,)),
            sems((HALVES * reps,)),
            sems((HALVES * reps,)),
            sems((HALVES * reps,)),
            sems((devices,)),
            sems((devices,)),
        ],
        compiler_params=pltpu.CompilerParams(
            collective_id=0, has_side_effects=True, vmem_limit_bytes=56 * 2**20
        ),
    )(
        entities,
        shared_table,
        edge_src,
        edge_dst,
        edge_slot,
        neg_rows,
        list_owner.reshape(list_row.shape),
        list_row,
        entity_state.reshape(1, share),
        shared_state.reshape(1, SH_DEV),
    )
    return (
        new_entities,
        new_entity_state.reshape(share),
        new_shared,
        new_shared_state.reshape(SH_DEV),
    )


def solution(mesh):
    return jax.shard_map(
        shards,
        mesh=mesh,
        in_specs=(
            P("blk", None),
            P(("blk", "rep")),
            P(),
            P(("blk", "rep")),
            P("blk", None, "rep"),
            P("blk", None, "rep"),
            P("blk", None, "rep"),
            P("blk", None, "rep", None),
            P("blk", "rep", None),
            P("blk", "rep"),
        ),
        out_specs=(
            P(("blk", "rep"), None),
            P(("blk", "rep")),
            P(("blk", "rep"), None),
            P(("blk", "rep")),
        ),
        check_vma=False,
    )
```
